512 devices in a mesh: ctx: 16 (over y, x_hi), req: 32 (over z, x_lo, core).
Axes of the slice: x: 4 (x_hi: 2, x_lo: 2; x = x_hi * 2 + x_lo), y: 8, z: 8, core: 2. Of those that a mesh axis runs over, the one named last changes fastest.
Arguments:
- queries: bfloat16 [196608, 2048], P(('ctx', 'req')), may hold values from -250 to 250
- suffix_keys: bfloat16 [196608, 512], P(('ctx', 'req')), may hold values from -6 to 6
- suffix_values: bfloat16 [196608, 512], P(('ctx', 'req')), may hold values from -6 to 6
- doc_keys: bfloat16 [2048, 512], P('ctx'), may hold values from -8 to 8
- doc_values: bfloat16 [2048, 512], P('ctx'), may hold values from -6 to 6
- lengths: int32 [1536], P(('ctx', 'req')), may hold values from 1 to 128
- targets: int32 [196608], P(('ctx', 'req')), may hold values from 0 to 31, as said below
Outputs:
- placed: bfloat16 [196608, 2048], P(('ctx', 'req'))
The draws below stay inside these ranges and needn't reach their ends.
Inputs may be any that keep to these rules, and one draw needn't show every extreme that they name: `targets`: among the 384 slots of each device, every value 0 to 32 - 1 occurs exactly 12 times.
All inputs are finite; a program needn't handle non-finite values.
Results may differ from the reference program's by a relative error of at most 0.013.
Values may be sent and summed in bfloat16 or wider, within the bound.
A program may use at most 128 MiB of HBM per device.

```python
import math
import jax
import jax.numpy as jnp
from jax import lax

HD = 128
KVH = 4
SUF = 128
REQ_DEV = 3
GROUPS = 4
QW = 2048
KVW = 512
TOK_DEV = 384
PER = 12
BLOCKS = 512
DOC = 2048
TOKENS = 196608
REQUESTS = 1536
N_REQ = 32


def shared_keys(key):
    return jax.random.normal(jax.random.fold_in(key, 5), (DOC, KVW), jnp.float32)


def draw_queries(key, part):
    key = jax.random.fold_in(key, 11)
    values = jax.random.normal(key, (TOKENS, QW), jnp.float32)
    return jnp.clip(values, -250.0, 250.0).astype(jnp.bfloat16)


def draw_doc_keys(key, part):
    common = shared_keys(key)
    values = common
    return jnp.clip(values, -8.0, 8.0).astype(jnp.bfloat16)


def draw_lengths(key, part):
    key = jax.random.fold_in(key, 13)
    counts = jax.random.randint(key, (REQUESTS,), 1, SUF + 1, dtype=jnp.int32)
    counts = counts.at[0].set(SUF)
    return counts.at[1].set(1)


def draw_targets(key, part):
    key = jax.random.fold_in(key, 14)
    pattern = jnp.arange(TOK_DEV, dtype=jnp.int32) % N_REQ
    streams = jax.random.split(key, BLOCKS)
    mixed = jax.vmap(lambda single: jax.random.permutation(single, pattern))(streams)
    return mixed.reshape(TOKENS).astype(jnp.int32)


def shard_levels(rng, dims, cuts, least, largest):
    level = 1.0
    for dim, shards_of in cuts:
        draws = jax.random.uniform(jax.random.fold_in(jax.random.fold_in(rng, 6), dim), (shards_of,), jnp.float32, least / len(cuts), largest / len(cuts))
        level = level * jnp.repeat(jnp.exp(draws), dims[dim] // shards_of).reshape((-1,) + (1,) * (len(dims) - 1 - dim))
    return level


def centred(own_key, dims, spread, bound, pieces=(), kind=jnp.bfloat16):
    level = shard_levels(own_key, dims, pieces, -0.22, 0.18) if pieces else 1.0
    array = jax.random.normal(own_key, dims, jnp.float32) * spread * level
    return jnp.minimum(jnp.maximum(array, -bound), bound).astype(kind)


def setup_inputs(seed: int = 0) -> dict:
    key_list = jax.random.split(jax.random.key(seed), 8)
    return {
        "queries": draw_queries(jax.random.fold_in(key_list[7], 71), 0),
        "suffix_keys": centred(key_list[1], (TOKENS, KVW), 1.0, 6.0, ((0, 512),)),
        "suffix_values": centred(key_list[2], (TOKENS, KVW), 1.0, 6.0, ((0, 512),)),
        "doc_keys": draw_doc_keys(jax.random.fold_in(key_list[7], 71), 0),
        "doc_values": centred(key_list[4], (DOC, KVW), 1.0, 6.0, ((0, 16),)),
        "lengths": draw_lengths(jax.random.fold_in(key_list[7], 71), 0),
        "targets": draw_targets(jax.random.fold_in(key_list[7], 71), 0),
    }


def reference(queries, suffix_keys, suffix_values, doc_keys, doc_values, lengths, targets):
    factor = 1.0 / math.sqrt(HD)
    doc_k = doc_keys.astype(jnp.float32).reshape(DOC, KVH, HD)
    doc_v = doc_values.astype(jnp.float32).reshape(DOC, KVH, HD)

    def one_block(inputs):
        query_rows, key_rows, value_rows, lens = inputs
        query_heads = query_rows.astype(jnp.float32).reshape(REQ_DEV, SUF, KVH, GROUPS, HD)
        key_heads = key_rows.astype(jnp.float32).reshape(REQ_DEV, SUF, KVH, HD)
        value_heads = value_rows.astype(jnp.float32).reshape(REQ_DEV, SUF, KVH, HD)
        scores = jnp.einsum('rtkgd,rukd->rkgtu', query_heads, key_heads) * factor
        causal = jnp.arange(SUF)[:, None] >= jnp.arange(SUF)[None, :]
        scores = jnp.where(causal, scores, -jnp.inf)
        high_s = lax.optimization_barrier(jnp.max(scores, axis=-1))
        weights = jnp.exp(scores - high_s[..., None])
        total_s = lax.optimization_barrier(jnp.sum(weights, axis=-1))
        summed_s = jnp.einsum('rkgtu,rukd->rtkgd', weights.astype(jnp.bfloat16).astype(jnp.float32), value_heads)
        normed_s = summed_s / jnp.transpose(total_s, (0, 3, 1, 2))[..., None]
        log_s = jnp.transpose(high_s + jnp.log(total_s), (0, 3, 1, 2))
        doc_scores = jnp.einsum('rtkgd,jkd->rtkgj', query_heads, doc_k) * factor
        high_d = lax.optimization_barrier(jnp.max(doc_scores, axis=-1))
        doc_weights = jnp.exp(doc_scores - high_d[..., None])
        total_d = lax.optimization_barrier(jnp.sum(doc_weights, axis=-1))
        summed_d = jnp.einsum('rtkgj,jkd->rtkgd', doc_weights.astype(jnp.bfloat16).astype(jnp.float32), doc_v)
        joint = jnp.logaddexp(log_s, high_d + jnp.log(total_d))
        result = jnp.exp(log_s - joint)[..., None] * normed_s + jnp.exp(high_d - joint)[..., None] * summed_d
        live_rows = jnp.arange(SUF)[None, :] < lens[:, None]
        result = jnp.where(live_rows[:, :, None, None, None], result, jnp.float32(0.0))
        return result.reshape(TOK_DEV, QW).astype(jnp.bfloat16)
    results = lax.map(one_block, (queries.reshape(BLOCKS, TOK_DEV, QW), suffix_keys.reshape(BLOCKS, TOK_DEV, KVW), suffix_values.reshape(BLOCKS, TOK_DEV, KVW), lengths.reshape(BLOCKS, REQ_DEV)))
    grouped = targets.reshape(BLOCKS, TOK_DEV)
    onehot = (grouped[..., None] == jnp.arange(N_REQ, dtype=jnp.int32)[None, None, :]).astype(jnp.int32)
    ranks = lax.optimization_barrier(jnp.sum(jnp.cumsum(onehot, axis=1) * onehot, axis=-1)) - 1
    device_ids = jnp.arange(BLOCKS, dtype=jnp.int32)[:, None]
    ctx_index = device_ids // N_REQ
    req_index = device_ids % N_REQ
    places = ((ctx_index * N_REQ + grouped) * TOK_DEV + req_index * PER + ranks).astype(jnp.int32)
    placed = jnp.zeros((TOKENS, QW), jnp.bfloat16).at[places.reshape(TOKENS)].set(results.reshape(TOKENS, QW))
    return placed
```

```python
import math

import jax
import jax.numpy as jnp
from jax import lax
from jax.experimental import pallas as pl
from jax.experimental.pallas import tpu as pltpu
from jax.sharding import PartitionSpec as P

HD = 128
KVH = 4
GROUPS = 4
SUF = 128
REQ_DEV = 3
TOK = 384
N_REQ = 32
PER = 12
TILE = 16
Y = 8
HALF = 64
SCALE = math.log2(math.e) / math.sqrt(HD)
NT = (((1,), (1,)), ((), ()))
MESH = pl.DeviceIdType.MESH
F32 = jnp.float32
BF16 = jnp.bfloat16
BLOCKS = ((0, 1), (1, 3), (3, 5), (5, 7), (7, 8))


def kernel(
    q_ref, sk_ref, sv_ref, dk_ref, dv_ref, len_ref, tgt_ref, out_ref,
    kv, vt, high, total, acc, res, pick, unpick, send, recv,
    ring_send, ring_recv, core_recv, ex_send, ex_recv,
):
    ctx, req = lax.axis_index("ctx"), lax.axis_index("req")
    y, xh = ctx // 2, ctx % 2
    z, quad = req // 4, req % 4
    xl, core = quad // 2, quad % 2
    up = ((y + 1) % Y) * 2 + xh
    down = ((y + Y - 1) % Y) * 2 + xh
    across = y * 2 + 1 - xh
    twin = req + 1 - 2 * core

    barrier = pltpu.get_barrier_semaphore()
    for other in (up, down, across):
        pl.semaphore_signal(barrier, inc=1, device_id=(other, req), device_id_type=MESH)

    @pl.loop(1, N_REQ)
    def _(s):
        pl.semaphore_signal(
            barrier, inc=1, device_id=(ctx, (req + s) % N_REQ), device_id_type=MESH
        )

    for g in range(KVH):
        lanes = slice(g * HD, (g + 1) * HD)
        for hf in range(2):
            start = core * HALF if hf == 0 else (1 - core) * HALF
            rows = pl.ds(pl.multiple_of(start, HALF), HALF)
            kv[0, g, 0, 0, hf] = dk_ref[rows, lanes]
            kv[1, g, 0, 0, hf] = dv_ref[rows, lanes]

    def ring(g, src, dst, st, other):
        pltpu.make_async_remote_copy(
            kv.at[:, g, src, st, 0], kv.at[:, g, dst, st, 0],
            ring_send.at[g], ring_recv.at[g, dst, st],
            device_id=(other, req), device_id_type=MESH,
        ).start()

    def pass_on(g, pos, st):
        pltpu.make_async_remote_copy(
            kv.at[:, g, pos, st, 0], kv.at[:, g, pos, st, 1],
            ring_send.at[g], core_recv.at[g, pos, st],
            device_id=(ctx, twin), device_id_type=MESH,
        ).start()

    def arrived(g, pos, st):
        part = kv.at[:, g, pos, st, 0]
        pltpu.make_async_copy(part, part, ring_recv.at[g, pos, st]).wait()

    def passed(g, pos, st):
        part = kv.at[:, g, pos, st, 1]
        pltpu.make_async_copy(part, part, core_recv.at[g, pos, st]).wait()

    def ring_start(g):
        ring(g, 0, 1, 0, up)
        ring(g, 0, 2, 0, down)
        pltpu.make_async_remote_copy(
            kv.at[:, g, 0, 0, 0], kv.at[:, g, 0, 1, 0],
            ring_send.at[g], ring_recv.at[g, 0, 1],
            device_id=(across, req), device_id_type=MESH,
        ).start()

    def ring_second(g):
        arrived(g, 0, 1)
        ring(g, 0, 1, 1, up)
        ring(g, 0, 2, 1, down)
        pass_on(g, 0, 1)

    def ring_stage(g, k):
        for st in range(2):
            if k == 4:
                arrived(g, 7, st)
                pass_on(g, 7, st)
                continue
            arrived(g, 2 * k - 1, st)
            if k < 3 or st == 0:
                ring(g, 2 * k - 1, 2 * k + 1, st, up)
            pass_on(g, 2 * k - 1, st)
            arrived(g, 2 * k, st)
            if k < 3:
                ring(g, 2 * k, 2 * k + 2, st, down)
            elif st == 1:
                ring(g, 2 * k, 7, st, down)
            pass_on(g, 2 * k, st)

    def whole(g, first, last):
        for pos in range(first, last):
            for st in range(2):
                if pos > 0 or st > 0:
                    passed(g, pos, st)

    def query(g, hh):
        return q_ref[:, pl.ds(pl.multiple_of((g * GROUPS + hh) * HD, HD), HD)]

    lower = lax.broadcasted_iota(jnp.int32, (SUF, SUF), 0) <= lax.broadcasted_iota(
        jnp.int32, (SUF, SUF), 1
    )

    def suffix(g, hh):
        q = query(g, hh)
        lanes = pl.ds(pl.multiple_of(g * HD, HD), HD)
        for r in range(REQ_DEV):
            rows = slice(r * SUF, (r + 1) * SUF)
            s = lax.dot_general(sk_ref[rows, lanes], q[rows], NT, preferred_element_type=F32)
            s = jnp.where(lower, s, -jnp.inf)
            top = jnp.max(s, axis=0, keepdims=True)
            p = jnp.exp2((s - top) * SCALE)
            high[hh, :, rows] = top
            total[hh, :, rows] = jnp.sum(p, axis=0, keepdims=True)
            acc[hh, :, rows] = jnp.dot(
                sv_ref[rows, lanes].T, p.astype(BF16), preferred_element_type=F32
            )

    def turn(g, first, last):
        n = (last - first) * 256
        v = kv[1, g, first:last].reshape(n, HD)
        vt[:, first * 256 : last * 256] = v.T

    def update(g, hh, first, last):
        n = (last - first) * 256
        keys = kv[0, g, first:last].reshape(n, HD)
        s = lax.dot_general(keys, query(g, hh), NT, preferred_element_type=F32)
        old = high[hh]
        top = jnp.maximum(old, jnp.max(s, axis=0, keepdims=True))
        decay = jnp.exp2((old - top) * SCALE)
        p = jnp.exp2((s - top) * SCALE)
        high[hh] = top
        total[hh] = total[hh] * decay + jnp.sum(p, axis=0, keepdims=True)
        acc[hh] = acc[hh] * decay + jnp.dot(
            vt[:, first * 256 : last * 256], p.astype(BF16), preferred_element_type=F32
        )

    lane = lax.broadcasted_iota(jnp.int32, (1, SUF), 1)
    live = jnp.concatenate([(lane < len_ref[r]).astype(F32) for r in range(REQ_DEV)], axis=1)

    def finish(hh):
        o = acc[hh] * (1.0 / total[hh])
        res[hh] = jnp.where(live > 0.0, o, 0.0).astype(BF16)

    def dispatch(g):
        for j in range(3):
            t = lax.dot_general(pick[0], res[j], NT, preferred_element_type=F32)
            t += lax.dot_general(pick[1 + j], res[3], NT, preferred_element_type=F32)
            send[g, :, j] = t.astype(BF16).reshape(N_REQ, TILE, HD)
        pltpu.make_async_copy(send.at[g, req], recv.at[g, req], ex_recv.at[g]).start()

        @pl.loop(0, N_REQ - 1)
        def _(s):
            j = s // 4
            step = (j // 2 + 1) * (1 - 2 * (j % 2)) + 4 * (j // 7)
            turned = s % 4 + s // 28
            x2, c2 = (xl + turned // 2) % 2, (core + turned) % 2
            dest = ((z + step + 8) % 8) * 4 + x2 * 2 + c2
            pltpu.make_async_remote_copy(
                send.at[g, dest], recv.at[g, req], ex_send.at[g], ex_recv.at[g],
                device_id=(ctx, dest), device_id_type=MESH,
            ).start()

    def collect(g):
        pltpu.make_async_copy(recv.at[g], recv.at[g], ex_recv.at[g]).wait()
        tiles = [recv[g, :, j].reshape(N_REQ * TILE, HD) for j in range(3)]
        last = None
        for j in range(3):
            lanes = slice((g * GROUPS + j) * HD, (g * GROUPS + j + 1) * HD)
            out_ref[:, lanes] = jnp.dot(unpick[0], tiles[j], preferred_element_type=F32).astype(BF16)
            t = jnp.dot(unpick[1 + j], tiles[j], preferred_element_type=F32)
            last = t if last is None else last + t
        out_ref[:, (g * GROUPS + 3) * HD : (g * GROUPS + 4) * HD] = last.astype(BF16)

    tgt = tgt_ref[...].reshape(1, TOK)
    mine = lax.broadcasted_iota(jnp.int32, (N_REQ, TOK), 0) == tgt
    before = lax.broadcasted_iota(jnp.int32, (TOK, TOK), 0) < lax.broadcasted_iota(
        jnp.int32, (TOK, TOK), 1
    )
    counts = jnp.dot(
        mine.astype(F32).astype(BF16), before.astype(F32).astype(BF16), preferred_element_type=F32
    )
    rank = jnp.sum(jnp.where(mine, counts, 0.0), axis=0, keepdims=True).astype(jnp.int32)
    row = lax.broadcasted_iota(jnp.int32, (N_REQ * TILE, TOK), 0)
    pick[0] = (row == tgt * TILE + rank).astype(F32).astype(BF16)
    spot = lax.broadcasted_iota(jnp.int32, (TOK, N_REQ * TILE), 1)
    place = lax.broadcasted_iota(jnp.int32, (TOK, N_REQ * TILE), 0)
    source, k = spot // TILE, spot % TILE
    unpick[0] = jnp.logical_and(place == source * PER + k, k < PER).astype(F32).astype(BF16)
    for j in range(3):
        inside = jnp.logical_and(rank >= 4 * j, rank < 4 * j + 4)
        code = jnp.where(inside, tgt * TILE + PER + rank - 4 * j, -1)
        pick[1 + j] = (row == code).astype(F32).astype(BF16)
        unpick[1 + j] = (
            jnp.logical_and(place == source * PER + 4 * j + k - PER, k >= PER)
            .astype(F32)
            .astype(BF16)
        )

    pl.semaphore_wait(barrier, N_REQ + 2)

    ring_start(0)

    @pl.loop(0, GROUPS)
    def _(hh):
        suffix(0, hh)

    ring_second(0)
    for k, (first, last) in enumerate(BLOCKS):
        if k < 4:
            ring_stage(0, k + 1)
        if k == 2:
            ring_start(1)
        if k == 3:
            ring_second(1)
            ring_stage(1, 1)
        if k == 4:
            ring_stage(1, 2)
        whole(0, first, last)
        turn(0, first, last)

        @pl.loop(0, GROUPS)
        def _(hh):
            update(0, hh, first, last)

    @pl.loop(0, GROUPS)
    def _(hh):
        finish(hh)

    dispatch(0)
    ring_stage(1, 3)

    @pl.loop(0, GROUPS)
    def _(hh):
        suffix(1, hh)

    ring_stage(1, 4)

    @pl.loop(1, KVH)
    def _(g):
        whole(g, 0, 8)
        turn(g, 0, 8)

        @pl.loop(0, GROUPS)
        def _(hh):
            @pl.when(g < KVH - 1)
            def _():
                @pl.when(hh == 0)
                def _():
                    ring_start(g + 1)

                @pl.when(hh == 1)
                def _():
                    ring_second(g + 1)
                    ring_stage(g + 1, 1)

                @pl.when(hh == 2)
                def _():
                    ring_stage(g + 1, 2)

                @pl.when(hh == 3)
                def _():
                    ring_stage(g + 1, 3)

            @pl.when(g > 1)
            def _():
                suffix(g, hh)

            update(g, hh, 0, 8)
            finish(hh)

        dispatch(g)

        @pl.when(g < KVH - 1)
        def _():
            ring_stage(g + 1, 4)

    for g in range(KVH):
        collect(g)
    for g in range(KVH):
        out = send.at[g, 0 : N_REQ - 1]
        pltpu.make_async_copy(out, out, ex_send.at[g]).wait()
        left = kv.at[:, 0:3, 0:5, :, 0]
        pltpu.make_async_copy(left, left, ring_send.at[g]).wait()


def body(queries, suffix_keys, suffix_values, doc_keys, doc_values, lengths, targets):
    vmem = pl.BlockSpec(memory_space=pltpu.VMEM)
    return pl.pallas_call(
        kernel,
        out_shape=jax.ShapeDtypeStruct((TOK, KVH * GROUPS * HD), BF16),
        in_specs=[vmem] * 5 + [pl.BlockSpec(memory_space=pltpu.SMEM), vmem],
        out_specs=vmem,
        scratch_shapes=[
            pltpu.VMEM((2, KVH, Y, 2, 2, HALF, HD), BF16),
            pltpu.VMEM((HD, Y * 256), BF16),
            pltpu.VMEM((GROUPS, 1, TOK), F32),
            pltpu.VMEM((GROUPS, 1, TOK), F32),
            pltpu.VMEM((GROUPS, HD, TOK), F32),
            pltpu.VMEM((GROUPS, HD, TOK), BF16),
            pltpu.VMEM((4, N_REQ * TILE, TOK), BF16),
            pltpu.VMEM((4, TOK, N_REQ * TILE), BF16),
            pltpu.VMEM((KVH, N_REQ, 3, TILE, HD), BF16),
            pltpu.VMEM((KVH, N_REQ, 3, TILE, HD), BF16),
            pltpu.SemaphoreType.DMA((KVH,)),
            pltpu.SemaphoreType.DMA((KVH, Y, 2)),
            pltpu.SemaphoreType.DMA((KVH, Y, 2)),
            pltpu.SemaphoreType.DMA((KVH,)),
            pltpu.SemaphoreType.DMA((KVH,)),
        ],
        compiler_params=pltpu.CompilerParams(
            collective_id=0, has_side_effects=True, vmem_limit_bytes=48 << 20
        ),
        cost_estimate=pl.CostEstimate(
            flops=7_000_000_000, bytes_accessed=4_000_000, transcendentals=13_000_000
        ),
    )(queries, suffix_keys, suffix_values, doc_keys, doc_values, lengths, targets)


def solution(mesh):
    both = P(("ctx", "req"), None)
    flat = P(("ctx", "req"))
    in_specs = (both, both, both, P("ctx", None), P("ctx", None), flat, flat)
    return jax.shard_map(body, mesh=mesh, in_specs=in_specs, out_specs=both, check_vma=False)
```

```python
import math

import jax
import jax.numpy as jnp
from jax import lax
from jax.experimental import pallas as pl
from jax.experimental.pallas import tpu as pltpu
from jax.sharding import PartitionSpec as P

HD = 128
KVH = 4
GROUPS = 4
SUF = 128
REQ_DEV = 3
TOK = 384
N_REQ = 32
PER = 12
TILE = 16
Y = 8
HALF = 64
SCALE = math.log2(math.e) / math.sqrt(HD)
NT = (((1,), (1,)), ((), ()))
MESH = pl.DeviceIdType.MESH
F32 = jnp.float32
BF16 = jnp.bfloat16
DOC = Y * 256
STEP = 256


def kernel(
    q_hbm, sk_hbm, sv_hbm, dk_hbm, dv_hbm, len_hbm, tgt_hbm, out_ref,
    q_ref, sk_ref, sv_ref, dk_ref, dv_ref, len_ref, tgt_ref,
    kv, vt, svt, s_ref, high, res, pick, unpick, send, recv,
    load_sem, ring_send, ring_recv, core_recv, ex_send, ex_recv,
):
    ctx, req = lax.axis_index("ctx"), lax.axis_index("req")
    y, xh = ctx // 2, ctx % 2
    z, quad = req // 4, req % 4
    xl, core = quad // 2, quad % 2
    steps = (0, 1, -1, 2, -2)

    def along(step, st):
        return ((y + step + Y) % Y) * 2 + (xh if st == 0 else 1 - xh)

    twin = req + 1 - 2 * core

    loads = [
        pltpu.make_async_copy(src, dst, load_sem.at[i])
        for i, (src, dst) in enumerate(
            (
                (dk_hbm, dk_ref), (dv_hbm, dv_ref), (tgt_hbm, tgt_ref), (len_hbm, len_ref),
                (q_hbm, q_ref), (sk_hbm, sk_ref), (sv_hbm, sv_ref),
            )
        )
    ]
    for load in loads:
        load.start()

    barrier = pltpu.get_barrier_semaphore()
    for st in range(2):
        for step in steps:
            if step != 0 or st != 0:
                pl.semaphore_signal(
                    barrier, inc=1, device_id=(along(step, st), req), device_id_type=MESH
                )

    @pl.loop(1, N_REQ)
    def _(s):
        pl.semaphore_signal(
            barrier, inc=1, device_id=(ctx, (req + s) % N_REQ), device_id_type=MESH
        )

    loads[0].wait()
    loads[1].wait()
    for g in range(KVH):
        lanes = slice(g * HD, (g + 1) * HD)
        for hf in range(2):
            start = core * HALF if hf == 0 else (1 - core) * HALF
            rows = pl.ds(pl.multiple_of(start, HALF), HALF)
            kv[0, g, 0, 0, hf] = dk_ref[rows, lanes]
            kv[1, g, 0, 0, hf] = dv_ref[rows, lanes]

    def ring(g, src, src_st, dst, st, other):
        pltpu.make_async_remote_copy(
            kv.at[:, g, src, src_st, 0], kv.at[:, g, dst, st, 0],
            ring_send.at[g], ring_recv.at[g, dst, st],
            device_id=(other, req), device_id_type=MESH,
        ).start()

    def pass_on(g, pos, st):
        pltpu.make_async_remote_copy(
            kv.at[:, g, pos, st, 0], kv.at[:, g, pos, st, 1],
            ring_send.at[g], core_recv.at[g, pos, st],
            device_id=(ctx, twin), device_id_type=MESH,
        ).start()

    def arrived(g, pos, st):
        part = kv.at[:, g, pos, st, 0]
        pltpu.make_async_copy(part, part, ring_recv.at[g, pos, st]).wait()

    def passed(g, pos, st):
        part = kv.at[:, g, pos, st, 1]
        pltpu.make_async_copy(part, part, core_recv.at[g, pos, st]).wait()

    def ring_start(g):
        for pos in (3, 4, 1, 2, 0):
            for st in range(2):
                if pos != 0 or st != 0:
                    ring(g, 0, 0, pos, st, along(steps[pos], st))

    def ring_relay(g):
        for st in range(2):
            arrived(g, 3, st)
            ring(g, 3, st, 5, st, along(1, 0))
            if st == 0:
                ring(g, 3, st, 7, st, along(2, 0))
            arrived(g, 4, st)
            ring(g, 4, st, 6, st, along(-1, 0))
            if st == 1:
                ring(g, 4, st, 7, st, along(-2, 0))
        for pos in range(5):
            for st in range(2):
                if pos in (1, 2) or (pos == 0 and st == 1):
                    arrived(g, pos, st)
                if pos != 0 or st != 0:
                    pass_on(g, pos, st)

    def ring_end(g):
        for pos in (5, 6, 7):
            for st in range(2):
                arrived(g, pos, st)
                pass_on(g, pos, st)

    def whole(g, first, last):
        for pos in range(first, last):
            for st in range(2):
                if pos > 0 or st > 0:
                    passed(g, pos, st)

    def query(g, hh):
        return q_ref[:, pl.ds(pl.multiple_of((g * GROUPS + hh) * HD, HD), HD)]

    lower = lax.broadcasted_iota(jnp.int32, (SUF, SUF), 0) <= lax.broadcasted_iota(
        jnp.int32, (SUF, SUF), 1
    )

    def key_lanes(g):
        return pl.ds(pl.multiple_of(g * HD, HD), HD)

    def suffix_scores(g, hh):
        q = query(g, hh)
        tops = []
        for r in range(REQ_DEV):
            rows = slice(r * SUF, (r + 1) * SUF)
            s = lax.dot_general(
                sk_ref[rows, key_lanes(g)], q[rows], NT, preferred_element_type=F32
            )
            s = jnp.where(lower, s, -jnp.inf)
            s_ref[hh, DOC:, rows] = s
            tops.append(jnp.max(s, axis=0, keepdims=True))
        return jnp.concatenate(tops, axis=1)

    def doc_scores(g, hh, first, last):
        n = (last - first) * 256
        keys = kv[0, g, first:last].reshape(n, HD)
        s = lax.dot_general(keys, query(g, hh), NT, preferred_element_type=F32)
        s_ref[hh, first * 256 : last * 256, :] = s
        return jnp.max(s, axis=0, keepdims=True)

    def turn(g, first, last):
        n = (last - first) * 256
        vt[:, first * 256 : last * 256] = kv[1, g, first:last].reshape(n, HD).T

    def attend(g, hh, top, ahead):
        total = summed = later = None
        for b in range(Y + 1):
            rows = slice(b * STEP, (b + 1) * STEP) if b < Y else slice(DOC, DOC + SUF)
            p = jnp.exp2((s_ref[hh, rows, :] - top) * SCALE)
            if ahead:
                t = doc_scores(g, hh + 1, b, b + 1) if b < Y else suffix_scores(g, hh + 1)
                later = t if later is None else jnp.maximum(later, t)
            t = jnp.sum(p, axis=0, keepdims=True)
            total = t if total is None else total + t
            p = p.astype(BF16)
            if b < Y:
                t = jnp.dot(vt[:, rows], p, preferred_element_type=F32)
            else:
                cols = [slice(r * SUF, (r + 1) * SUF) for r in range(REQ_DEV)]
                t = jnp.concatenate(
                    [jnp.dot(svt[:, c], p[:, c], preferred_element_type=F32) for c in cols], axis=1
                )
            summed = t if summed is None else summed + t
        o = summed * (1.0 / total)
        res[hh] = jnp.where(live > 0.0, o, 0.0).astype(BF16)
        return later

    for load in loads[2:4]:
        load.wait()
    lane = lax.broadcasted_iota(jnp.int32, (1, SUF), 1)
    live = jnp.concatenate([(lane < len_ref[r]).astype(F32) for r in range(REQ_DEV)], axis=1)

    def dispatch(g):
        for j in range(3):
            t = lax.dot_general(pick[0], res[j], NT, preferred_element_type=F32)
            t += lax.dot_general(pick[1 + j], res[3], NT, preferred_element_type=F32)
            send[g, :, j] = t.astype(BF16).reshape(N_REQ, TILE, HD)
        pltpu.make_async_copy(send.at[g, req], recv.at[g, req], ex_recv.at[g]).start()

        @pl.loop(0, N_REQ - 1)
        def _(s):
            j = s // 4
            step = (j // 2 + 1) * (1 - 2 * (j % 2)) + 4 * (j // 7)
            turned = s % 4 + s // 28
            x2, c2 = (xl + turned // 2) % 2, (core + turned) % 2
            dest = ((z + step + 8) % 8) * 4 + x2 * 2 + c2
            pltpu.make_async_remote_copy(
                send.at[g, dest], recv.at[g, req], ex_send.at[g], ex_recv.at[g],
                device_id=(ctx, dest), device_id_type=MESH,
            ).start()

    def collect(g):
        pltpu.make_async_copy(recv.at[g], recv.at[g], ex_recv.at[g]).wait()
        tiles = [recv[g, :, j].reshape(N_REQ * TILE, HD) for j in range(3)]
        last = None
        for j in range(3):
            lanes = slice((g * GROUPS + j) * HD, (g * GROUPS + j + 1) * HD)
            out_ref[:, lanes] = jnp.dot(unpick[0], tiles[j], preferred_element_type=F32).astype(BF16)
            t = jnp.dot(unpick[1 + j], tiles[j], preferred_element_type=F32)
            last = t if last is None else last + t
        out_ref[:, (g * GROUPS + 3) * HD : (g * GROUPS + 4) * HD] = last.astype(BF16)

    tgt = tgt_ref[...].reshape(1, TOK)
    mine = lax.broadcasted_iota(jnp.int32, (N_REQ, TOK), 0) == tgt
    before = lax.broadcasted_iota(jnp.int32, (TOK, TOK), 0) < lax.broadcasted_iota(
        jnp.int32, (TOK, TOK), 1
    )
    counts = jnp.dot(
        mine.astype(F32).astype(BF16), before.astype(F32).astype(BF16), preferred_element_type=F32
    )
    rank = jnp.sum(jnp.where(mine, counts, 0.0), axis=0, keepdims=True).astype(jnp.int32)
    row = lax.broadcasted_iota(jnp.int32, (N_REQ * TILE, TOK), 0)
    pick[0] = (row == tgt * TILE + rank).astype(F32).astype(BF16)
    spot = lax.broadcasted_iota(jnp.int32, (TOK, N_REQ * TILE), 1)
    place = lax.broadcasted_iota(jnp.int32, (TOK, N_REQ * TILE), 0)
    source, k = spot // TILE, spot % TILE
    unpick[0] = jnp.logical_and(place == source * PER + k, k < PER).astype(F32).astype(BF16)
    for j in range(3):
        inside = jnp.logical_and(rank >= 4 * j, rank < 4 * j + 4)
        code = jnp.where(inside, tgt * TILE + PER + rank - 4 * j, -1)
        pick[1 + j] = (row == code).astype(F32).astype(BF16)
        unpick[1 + j] = (
            jnp.logical_and(place == source * PER + 4 * j + k - PER, k >= PER)
            .astype(F32)
            .astype(BF16)
        )

    pl.semaphore_wait(barrier, N_REQ - 1 + 9)
    ring_start(0)
    for load in loads[4:]:
        load.wait()

    @pl.loop(0, GROUPS)
    def _(hh):
        high[hh] = suffix_scores(0, hh)

    ring_relay(0)
    ring_start(1)
    for first, last in ((0, 5), (5, Y)):
        if first > 0:
            ring_end(0)
        whole(0, first, last)
        turn(0, first, last)

        @pl.loop(0, GROUPS)
        def _(hh):
            high[hh] = jnp.maximum(high[hh], doc_scores(0, hh, first, last))

    def hooks(g, tick):
        def when(cond, act):
            if isinstance(g, int):
                if cond:
                    act()
            else:
                pl.when(cond)(act)

        if tick == 2:
            when(g + 1 < KVH, lambda: ring_relay(g + 1))
        if tick == 3:
            when(g + 2 < KVH, lambda: ring_start(g + 2))
        if tick == 4:
            when(g + 1 < KVH, lambda: ring_end(g + 1))

    svt[...] = sv_ref[:, 0:HD].T
    for hh in range(GROUPS):
        hooks(0, hh)
        attend(0, hh, high[hh], False)
    dispatch(0)
    hooks(0, 4)

    @pl.loop(1, KVH)
    def _(g):
        whole(g, 0, 8)
        turn(g, 0, 8)
        svt[...] = sv_ref[:, key_lanes(g)].T
        top = suffix_scores(g, 0)
        for b in range(Y):
            top = jnp.maximum(top, doc_scores(g, 0, b, b + 1))
        for hh in range(GROUPS):
            hooks(g, hh)
            top = attend(g, hh, top, hh < GROUPS - 1)
        dispatch(g)
        hooks(g, 4)

    for g in range(KVH):
        collect(g)
    for g in range(KVH):
        out = send.at[g, 0 : N_REQ - 1]
        pltpu.make_async_copy(out, out, ex_send.at[g]).wait()
        left = kv.at[:, 0:3, 0:5, :, 0]
        pltpu.make_async_copy(left, left, ring_send.at[g]).wait()


def body(queries, suffix_keys, suffix_values, doc_keys, doc_values, lengths, targets):
    vmem = pl.BlockSpec(memory_space=pltpu.VMEM)
    hbm = pl.BlockSpec(memory_space=pl.ANY)
    return pl.pallas_call(
        kernel,
        out_shape=jax.ShapeDtypeStruct((TOK, KVH * GROUPS * HD), BF16),
        in_specs=[hbm] * 7,
        out_specs=vmem,
        scratch_shapes=[
            pltpu.VMEM((TOK, KVH * GROUPS * HD), BF16),
            pltpu.VMEM((TOK, KVH * HD), BF16),
            pltpu.VMEM((TOK, KVH * HD), BF16),
            pltpu.VMEM((SUF, KVH * HD), BF16),
            pltpu.VMEM((SUF, KVH * HD), BF16),
            pltpu.SMEM((REQ_DEV,), jnp.int32),
            pltpu.VMEM((TOK,), jnp.int32),
            pltpu.VMEM((2, KVH, Y, 2, 2, HALF, HD), BF16),
            pltpu.VMEM((HD, DOC), BF16),
            pltpu.VMEM((HD, TOK), BF16),
            pltpu.VMEM((GROUPS, DOC + SUF, TOK), F32),
            pltpu.VMEM((GROUPS, 1, TOK), F32),
            pltpu.VMEM((GROUPS, HD, TOK), BF16),
            pltpu.VMEM((4, N_REQ * TILE, TOK), BF16),
            pltpu.VMEM((4, TOK, N_REQ * TILE), BF16),
            pltpu.VMEM((KVH, N_REQ, 3, TILE, HD), BF16),
            pltpu.VMEM((KVH, N_REQ, 3, TILE, HD), BF16),
            pltpu.SemaphoreType.DMA((7,)),
            pltpu.SemaphoreType.DMA((KVH,)),
            pltpu.SemaphoreType.DMA((KVH, Y, 2)),
            pltpu.SemaphoreType.DMA((KVH, Y, 2)),
            pltpu.SemaphoreType.DMA((KVH,)),
            pltpu.SemaphoreType.DMA((KVH,)),
        ],
        compiler_params=pltpu.CompilerParams(
            collective_id=0, has_side_effects=True, vmem_limit_bytes=56 << 20
        ),
        cost_estimate=pl.CostEstimate(
            flops=7_000_000_000, bytes_accessed=4_000_000, transcendentals=13_000_000
        ),
    )(queries, suffix_keys, suffix_values, doc_keys, doc_values, lengths, targets)


def solution(mesh):
    both = P(("ctx", "req"), None)
    flat = P(("ctx", "req"))
    in_specs = (both, both, both, P("ctx", None), P("ctx", None), flat, flat)
    return jax.shard_map(body, mesh=mesh, in_specs=in_specs, out_specs=both, check_vma=False)
```

```python
import math

import jax
import jax.numpy as jnp
from jax import lax
from jax.experimental import pallas as pl
from jax.experimental.pallas import tpu as pltpu
from jax.sharding import PartitionSpec as P

HD = 128
KVH = 4
GROUPS = 4
SUF = 128
REQ_DEV = 3
TOK = 384
N_REQ = 32
PER = 12
TILE = 16
Y = 8
HALF = 64
SCALE = math.log2(math.e) / math.sqrt(HD)
NT = (((1,), (1,)), ((), ()))
MESH = pl.DeviceIdType.MESH
F32 = jnp.float32
BF16 = jnp.bfloat16
DOC = Y * 256
STEP = 256


def kernel(
    q_hbm, sk_hbm, sv_hbm, dk_hbm, dv_hbm, len_hbm, tgt_hbm, out_ref,
    q_ref, sk_ref, sv_ref, dk_ref, dv_ref, len_ref, tgt_ref,
    kv, vt, svt, s_ref, high, res, pick, unpick, send, recv,
    load_sem, ring_send, ring_recv, core_recv, ex_send, ex_recv,
):
    ctx, req = lax.axis_index("ctx"), lax.axis_index("req")
    y, xh = ctx // 2, ctx % 2
    z, quad = req // 4, req % 4
    xl, core = quad // 2, quad % 2
    steps = (0, 1, -1, 2, -2)

    def along(step, st):
        return ((y + step + Y) % Y) * 2 + (xh if st == 0 else 1 - xh)

    twin = req + 1 - 2 * core

    loads = [
        pltpu.make_async_copy(src, dst, load_sem.at[i])
        for i, (src, dst) in enumerate(
            (
                (dk_hbm, dk_ref), (dv_hbm, dv_ref), (tgt_hbm, tgt_ref), (len_hbm, len_ref),
                (q_hbm, q_ref), (sk_hbm, sk_ref), (sv_hbm, sv_ref),
            )
        )
    ]
    for load in loads:
        load.start()

    barrier = pltpu.get_barrier_semaphore()
    for st in range(2):
        for step in steps:
            if step != 0 or st != 0:
                pl.semaphore_signal(
                    barrier, inc=1, device_id=(along(step, st), req), device_id_type=MESH
                )

    @pl.loop(1, N_REQ)
    def _(s):
        pl.semaphore_signal(
            barrier, inc=1, device_id=(ctx, (req + s) % N_REQ), device_id_type=MESH
        )

    loads[0].wait()
    loads[1].wait()
    for g in range(KVH):
        lanes = slice(g * HD, (g + 1) * HD)
        for hf in range(2):
            start = core * HALF if hf == 0 else (1 - core) * HALF
            rows = pl.ds(pl.multiple_of(start, HALF), HALF)
            kv[0, g, 0, 0, hf] = dk_ref[rows, lanes]
            kv[1, g, 0, 0, hf] = dv_ref[rows, lanes]

    def ring(g, src, src_st, dst, st, other):
        pltpu.make_async_remote_copy(
            kv.at[:, g, src, src_st, 0], kv.at[:, g, dst, st, 0],
            ring_send.at[g], ring_recv.at[g, dst, st],
            device_id=(other, req), device_id_type=MESH,
        ).start()

    def pass_on(g, pos, st):
        pltpu.make_async_remote_copy(
            kv.at[:, g, pos, st, 0], kv.at[:, g, pos, st, 1],
            ring_send.at[g], core_recv.at[g, pos, st],
            device_id=(ctx, twin), device_id_type=MESH,
        ).start()

    def arrived(g, pos, st):
        part = kv.at[:, g, pos, st, 0]
        pltpu.make_async_copy(part, part, ring_recv.at[g, pos, st]).wait()

    def passed(g, pos, st):
        part = kv.at[:, g, pos, st, 1]
        pltpu.make_async_copy(part, part, core_recv.at[g, pos, st]).wait()

    def ring_start(g):
        for pos in (3, 4, 1, 2, 0):
            for st in range(2):
                if pos != 0 or st != 0:
                    ring(g, 0, 0, pos, st, along(steps[pos], st))

    def ring_relay(g):
        for st in range(2):
            arrived(g, 3, st)
            ring(g, 3, st, 5, st, along(1, 0))
            if st == 0:
                ring(g, 3, st, 7, st, along(2, 0))
            arrived(g, 4, st)
            ring(g, 4, st, 6, st, along(-1, 0))
            if st == 1:
                ring(g, 4, st, 7, st, along(-2, 0))
        for pos in range(5):
            for st in range(2):
                if pos in (1, 2) or (pos == 0 and st == 1):
                    arrived(g, pos, st)
                if pos != 0 or st != 0:
                    pass_on(g, pos, st)

    def ring_end(g):
        for pos in (5, 6, 7):
            for st in range(2):
                arrived(g, pos, st)
                pass_on(g, pos, st)

    def whole(g, first, last):
        for pos in range(first, last):
            for st in range(2):
                if pos > 0 or st > 0:
                    passed(g, pos, st)

    def query(g, hh):
        return q_ref[:, pl.ds(pl.multiple_of((g * GROUPS + hh) * HD, HD), HD)]

    lower = lax.broadcasted_iota(jnp.int32, (SUF, SUF), 0) <= lax.broadcasted_iota(
        jnp.int32, (SUF, SUF), 1
    )

    def key_lanes(g):
        return pl.ds(pl.multiple_of(g * HD, HD), HD)

    def suffix_scores(g, hh):
        q = query(g, hh)
        tops = []
        for r in range(REQ_DEV):
            rows = slice(r * SUF, (r + 1) * SUF)
            s = lax.dot_general(
                sk_ref[rows, key_lanes(g)], q[rows], NT, preferred_element_type=F32
            )
            s = jnp.where(lower, s, -jnp.inf)
            s_ref[hh, DOC:, rows] = s
            tops.append(jnp.max(s, axis=0, keepdims=True))
        return jnp.concatenate(tops, axis=1)

    def doc_scores(g, hh, first, last):
        n = (last - first) * 256
        keys = kv[0, g, first:last].reshape(n, HD)
        s = lax.dot_general(keys, query(g, hh), NT, preferred_element_type=F32)
        s_ref[hh, first * 256 : last * 256, :] = s
        return jnp.max(s, axis=0, keepdims=True)

    def turn(g, first, last):
        n = (last - first) * 256
        vt[:, first * 256 : last * 256] = kv[1, g, first:last].reshape(n, HD).T

    def attend(g, hh, top, ahead):
        total = summed = later = None
        for b in range(Y + 1):
            rows = slice(b * STEP, (b + 1) * STEP) if b < Y else slice(DOC, DOC + SUF)
            p = jnp.exp2((s_ref[hh, rows, :] - top) * SCALE)
            if ahead:
                t = doc_scores(g, hh + 1, b, b + 1) if b < Y else suffix_scores(g, hh + 1)
                later = t if later is None else jnp.maximum(later, t)
            t = jnp.sum(p, axis=0, keepdims=True)
            total = t if total is None else total + t
            p = p.astype(BF16)
            if b < Y:
                t = jnp.dot(vt[:, rows], p, preferred_element_type=F32)
            else:
                cols = [slice(r * SUF, (r + 1) * SUF) for r in range(REQ_DEV)]
                t = jnp.concatenate(
                    [jnp.dot(svt[:, c], p[:, c], preferred_element_type=F32) for c in cols], axis=1
                )
            summed = t if summed is None else summed + t
        o = summed * (1.0 / total)
        res[hh] = jnp.where(live > 0.0, o, 0.0).astype(BF16)
        return later

    for load in loads[2:4]:
        load.wait()
    lane = lax.broadcasted_iota(jnp.int32, (1, SUF), 1)
    live = jnp.concatenate([(lane < len_ref[r]).astype(F32) for r in range(REQ_DEV)], axis=1)

    def dispatch(g):
        for j in range(3):
            t = lax.dot_general(pick[0], res[j], NT, preferred_element_type=F32)
            t += lax.dot_general(pick[1 + j], res[3], NT, preferred_element_type=F32)
            send[g, :, j] = t.astype(BF16).reshape(N_REQ, TILE, HD)
        pltpu.make_async_copy(send.at[g, req], recv.at[g, req], ex_recv.at[g]).start()

        @pl.loop(0, N_REQ - 1)
        def _(s):
            j = s // 4
            step = (j // 2 + 1) * (1 - 2 * (j % 2)) + 4 * (j // 7)
            turned = s % 4 + s // 28
            x2, c2 = (xl + turned // 2) % 2, (core + turned) % 2
            dest = ((z + step + 8) % 8) * 4 + x2 * 2 + c2
            pltpu.make_async_remote_copy(
                send.at[g, dest], recv.at[g, req], ex_send.at[g], ex_recv.at[g],
                device_id=(ctx, dest), device_id_type=MESH,
            ).start()

    def collect(g):
        pltpu.make_async_copy(recv.at[g], recv.at[g], ex_recv.at[g]).wait()
        tiles = [recv[g, :, j].reshape(N_REQ * TILE, HD) for j in range(3)]
        last = None
        for j in range(3):
            lanes = slice((g * GROUPS + j) * HD, (g * GROUPS + j + 1) * HD)
            out_ref[:, lanes] = jnp.dot(unpick[0], tiles[j], preferred_element_type=F32).astype(BF16)
            t = jnp.dot(unpick[1 + j], tiles[j], preferred_element_type=F32)
            last = t if last is None else last + t
        out_ref[:, (g * GROUPS + 3) * HD : (g * GROUPS + 4) * HD] = last.astype(BF16)

    tgt = tgt_ref[...].reshape(1, TOK)
    mine = lax.broadcasted_iota(jnp.int32, (N_REQ, TOK), 0) == tgt
    before = lax.broadcasted_iota(jnp.int32, (TOK, TOK), 0) < lax.broadcasted_iota(
        jnp.int32, (TOK, TOK), 1
    )
    counts = jnp.dot(
        mine.astype(F32).astype(BF16), before.astype(F32).astype(BF16), preferred_element_type=F32
    )
    rank = jnp.sum(jnp.where(mine, counts, 0.0), axis=0, keepdims=True).astype(jnp.int32)
    row = lax.broadcasted_iota(jnp.int32, (N_REQ * TILE, TOK), 0)
    pick[0] = (row == tgt * TILE + rank).astype(F32).astype(BF16)
    spot = lax.broadcasted_iota(jnp.int32, (TOK, N_REQ * TILE), 1)
    place = lax.broadcasted_iota(jnp.int32, (TOK, N_REQ * TILE), 0)
    source, k = spot // TILE, spot % TILE
    unpick[0] = jnp.logical_and(place == source * PER + k, k < PER).astype(F32).astype(BF16)
    for j in range(3):
        inside = jnp.logical_and(rank >= 4 * j, rank < 4 * j + 4)
        code = jnp.where(inside, tgt * TILE + PER + rank - 4 * j, -1)
        pick[1 + j] = (row == code).astype(F32).astype(BF16)
        unpick[1 + j] = (
            jnp.logical_and(place == source * PER + 4 * j + k - PER, k >= PER)
            .astype(F32)
            .astype(BF16)
        )

    pl.semaphore_wait(barrier, N_REQ - 1 + 9)
    ring_start(0)
    for load in loads[4:]:
        load.wait()

    @pl.loop(0, GROUPS)
    def _(hh):
        high[hh] = suffix_scores(0, hh)

    ring_relay(0)
    ring_start(1)
    ring_start(2)
    for first, last in ((0, 5), (5, Y)):
        if first > 0:
            ring_end(0)
        whole(0, first, last)
        turn(0, first, last)

        @pl.loop(0, GROUPS)
        def _(hh):
            high[hh] = jnp.maximum(high[hh], doc_scores(0, hh, first, last))

    def hooks(g, tick):
        def when(cond, act):
            if isinstance(g, int):
                if cond:
                    act()
            else:
                pl.when(cond)(act)

        if tick == 0:
            when(g + 1 < KVH, lambda: ring_relay(g + 1))
        if tick == 1:
            when(g + 3 < KVH, lambda: ring_start(g + 3))
        if tick == 4:
            when(g + 1 < KVH, lambda: ring_end(g + 1))

    svt[...] = sv_ref[:, 0:HD].T
    for hh in range(GROUPS):
        hooks(0, hh)
        attend(0, hh, high[hh], False)
    dispatch(0)
    hooks(0, 4)

    @pl.loop(1, KVH)
    def _(g):
        whole(g, 0, 8)
        turn(g, 0, 8)
        svt[...] = sv_ref[:, key_lanes(g)].T
        top = suffix_scores(g, 0)
        for b in range(Y):
            top = jnp.maximum(top, doc_scores(g, 0, b, b + 1))
        for hh in range(GROUPS):
            hooks(g, hh)
            top = attend(g, hh, top, hh < GROUPS - 1)
        dispatch(g)
        hooks(g, 4)

    for g in range(KVH):
        collect(g)
    for g in range(KVH):
        out = send.at[g, 0 : N_REQ - 1]
        pltpu.make_async_copy(out, out, ex_send.at[g]).wait()
        left = kv.at[:, 0:3, 0:5, :, 0]
        pltpu.make_async_copy(left, left, ring_send.at[g]).wait()


def body(queries, suffix_keys, suffix_values, doc_keys, doc_values, lengths, targets):
    vmem = pl.BlockSpec(memory_space=pltpu.VMEM)
    hbm = pl.BlockSpec(memory_space=pl.ANY)
    return pl.pallas_call(
        kernel,
        out_shape=jax.ShapeDtypeStruct((TOK, KVH * GROUPS * HD), BF16),
        in_specs=[hbm] * 7,
        out_specs=vmem,
        scratch_shapes=[
            pltpu.VMEM((TOK, KVH * GROUPS * HD), BF16),
            pltpu.VMEM((TOK, KVH * HD), BF16),
            pltpu.VMEM((TOK, KVH * HD), BF16),
            pltpu.VMEM((SUF, KVH * HD), BF16),
            pltpu.VMEM((SUF, KVH * HD), BF16),
            pltpu.SMEM((REQ_DEV,), jnp.int32),
            pltpu.VMEM((TOK,), jnp.int32),
            pltpu.VMEM((2, KVH, Y, 2, 2, HALF, HD), BF16),
            pltpu.VMEM((HD, DOC), BF16),
            pltpu.VMEM((HD, TOK), BF16),
            pltpu.VMEM((GROUPS, DOC + SUF, TOK), F32),
            pltpu.VMEM((GROUPS, 1, TOK), F32),
            pltpu.VMEM((GROUPS, HD, TOK), BF16),
            pltpu.VMEM((4, N_REQ * TILE, TOK), BF16),
            pltpu.VMEM((4, TOK, N_REQ * TILE), BF16),
            pltpu.VMEM((KVH, N_REQ, 3, TILE, HD), BF16),
            pltpu.VMEM((KVH, N_REQ, 3, TILE, HD), BF16),
            pltpu.SemaphoreType.DMA((7,)),
            pltpu.SemaphoreType.DMA((KVH,)),
            pltpu.SemaphoreType.DMA((KVH, Y, 2)),
            pltpu.SemaphoreType.DMA((KVH, Y, 2)),
            pltpu.SemaphoreType.DMA((KVH,)),
            pltpu.SemaphoreType.DMA((KVH,)),
        ],
        compiler_params=pltpu.CompilerParams(
            collective_id=0, has_side_effects=True, vmem_limit_bytes=56 << 20
        ),
        cost_estimate=pl.CostEstimate(
            flops=7_000_000_000, bytes_accessed=4_000_000, transcendentals=13_000_000
        ),
    )(queries, suffix_keys, suffix_values, doc_keys, doc_values, lengths, targets)


def solution(mesh):
    both = P(("ctx", "req"), None)
    flat = P(("ctx", "req"))
    in_specs = (both, both, both, P("ctx", None), P("ctx", None), flat, flat)
    return jax.shard_map(body, mesh=mesh, in_specs=in_specs, out_specs=both, check_vma=False)
```
